32 devices in a mesh: tgt: 8 (over y, x, core), src: 4 (over z).
Axes of the slice: x: 2, y: 2, z: 4, core: 2. Of those that a mesh axis runs over, the one named last changes fastest.
Arguments:
- targets: float32 [8, 64, 4096], P('tgt'), may hold values from -8 to 8
- sources: float32 [8, 64, 4096], P('src', 'tgt'), may hold values from -8 to 8
- occupations: float32 [8], P('src'), may hold values from 0.2 to 2
Outputs:
- exchange_term: float32 [8, 64, 4096], P('tgt', 'src')
The draws below stay inside these ranges and needn't reach their ends.
All inputs are finite; a program needn't handle non-finite values.
Results may differ from the reference program's by a relative error of at most 0.000076.
Values sent between devices are 32-bit elements; how exact they have to be, the bound alone decides.
A program may use at most 64 MiB of HBM per device.

```python
import math
import jax
import jax.numpy as jnp
from jax import lax

G = 64
NT = 8
NS = 8


def orbital_field(key, count, salt):
    key = jax.random.fold_in(key, salt)
    first, second = jax.random.split(key, 2)
    scales = jnp.exp(jax.random.uniform(first, (count, 1, 1), jnp.float32, math.log(0.5), math.log(2.0)))
    rough = jax.random.normal(second, (count, G, G * G), jnp.float32) * scales
    return jnp.clip(rough, -8.0, 8.0).astype(jnp.float32)


def draw_targets(key, part):
    return orbital_field(key, NT, 11)


def draw_sources(key, part):
    return orbital_field(key, NS, 23)


def block_scale(stream_key, extent, cuts, least, largest):
    gain, own = 1.0, jax.random.fold_in(stream_key, 6)
    for axis_at, shards_of in cuts:
        steps = jnp.exp(jax.random.uniform(jax.random.fold_in(own, axis_at), (shards_of,), jnp.float32, least / len(cuts), largest / len(cuts)))
        gain = gain * jnp.repeat(steps, extent[axis_at] // shards_of).reshape([-1 if axis == axis_at else 1 for axis in range(len(extent))])
    return gain


def setup_inputs(seed: int = 0) -> dict:
    streams_of = jax.random.split(jax.random.key(seed), 4)
    return {
        "targets": draw_targets(jax.random.fold_in(streams_of[3], 71), 0),
        "sources": draw_sources(jax.random.fold_in(streams_of[3], 71), 0),
        "occupations": jnp.clip(jnp.exp(math.log(2.0) - 2.3025851 * jax.random.uniform(streams_of[2], (NS,), jnp.float32) ** block_scale(streams_of[2], (NS,), ((0, 4),), -0.2, 0.2)), 0.2, 2.0),
    }


def kernel_grid(size):
    freq = ((jnp.arange(size, dtype=jnp.int32) + size // 2) % size - size // 2).astype(jnp.float32)
    square = freq[:, None, None] ** 2 + freq[None, :, None] ** 2 + freq[None, None, :] ** 2
    return 16.0 / (square + 0.25)


def reference(targets, sources, occupations):
    size = targets.shape[1]
    count = sources.shape[0]
    kernel = kernel_grid(size)
    source_grid = sources.reshape(count, size, size, size)
    weighted = occupations[:, None, None, None] * source_grid

    def one_target(target):
        pair = target.reshape(size, size, size)[None] * source_grid
        spectrum = jnp.fft.fftn(pair, axes=(1, 2, 3))
        potential = jnp.real(jnp.fft.ifftn(kernel[None] * spectrum, axes=(1, 2, 3)))
        total = -jnp.sum(weighted * potential, axis=0)
        return total.reshape(size, size * size)

    return lax.map(one_target, targets)
```

```python
import functools
import math

import jax
import jax.numpy as jnp
import ml_dtypes
import numpy as np
from jax import lax
from jax.experimental import pallas as pl
from jax.experimental.pallas import tpu as pltpu
from jax.sharding import PartitionSpec as P

MESH = pl.DeviceIdType.MESH
LANES = 128


def split_table(table):
    high = table.astype(np.float32).astype(ml_dtypes.bfloat16)
    low = (table - high.astype(np.float64)).astype(np.float32).astype(ml_dtypes.bfloat16)
    return high, low


def basis(size):
    half = size // 2
    point = np.arange(size)
    freq = np.where(point <= half, point, point - half)
    angle = (freq[:, None] * point[None, :] % size) * (2.0 * math.pi / size)
    rows = np.where((point <= half)[:, None], np.cos(angle), np.sin(angle))
    norm = np.where((freq == 0) | (freq == half), 1.0, 2.0) / size
    return rows * np.sqrt(norm)[:, None], freq


def tables(size, count):
    rows, freq = basis(size)
    fold = LANES // size

    def left(matrix):
        high, low = split_table(matrix)
        return np.concatenate([high, high, low], axis=1)

    wide = np.zeros((count, fold, size, fold, count, size))
    for p in range(count):
        for y in range(fold):
            wide[p, y, :, y, p, :] = rows.T
    wide = wide.reshape(count * LANES, count * LANES)
    half = np.arange(size // 2 + 1).astype(np.float64)
    square = half[:, None, None] ** 2 + freq[None, :, None] ** 2 + freq[None, None, :] ** 2
    kern = (16.0 / (square + 0.25)).astype(np.float32)
    kern = np.concatenate([kern] * count, axis=-1)
    forward, inverse = split_table(wide), split_table(wide.T.copy())
    return left(rows), left(rows.T.copy()), *forward, *inverse, kern


def halves(value):
    high = value.astype(jnp.bfloat16)
    low = (value - high.astype(jnp.float32)).astype(jnp.bfloat16)
    return high, low


def dot(a, b):
    return jnp.dot(a, b, preferred_element_type=jnp.float32)


def from_left(table, value):
    high, low = halves(value)
    return dot(table, jnp.concatenate([high, low, high], axis=0))


def from_right(value, table_high, table_low):
    high, low = halves(value)
    return dot(high, table_high) + dot(low, table_high) + dot(high, table_low)


def body(shape, tgt, src, occ, left_f, left_i, right_fh, right_fl, right_ih, right_il, kern, out,
         whole, field, part, from_low, from_high, own_sem, send_sem, recv_sem, sum_send, low_recv, high_recv):
    nt, ns, count, size, chunks = shape
    width = size * size
    cut = width // chunks
    blocks = cut // LANES
    fold = LANES // size
    rows = part.shape[1]
    me, here = lax.axis_index("tgt"), lax.axis_index("src")
    chips = nt // 2
    chip, core = me // 2, me % 2
    mate = chip * 2 + (1 - core)

    def peer(step):
        return lax.rem(chip + step + chips, chips) * 2 + core

    barrier = pltpu.get_barrier_semaphore()
    for step in range(1, chips):
        pl.semaphore_signal(barrier, inc=1, device_id={"tgt": peer(step)}, device_id_type=MESH)
    pl.semaphore_signal(barrier, inc=1, device_id={"tgt": mate}, device_id_type=MESH)

    @pl.when(here > 0)
    def _():
        pl.semaphore_signal(barrier, inc=1, device_id={"src": here - 1}, device_id_type=MESH)

    @pl.when(here < ns - 1)
    def _():
        pl.semaphore_signal(barrier, inc=1, device_id={"src": here + 1}, device_id_type=MESH)

    own = pltpu.make_async_copy(src, whole.at[me], own_sem)
    own.start()
    inner = jnp.where(here > 0, 1, 0) + jnp.where(here < ns - 1, 1, 0)
    pl.semaphore_wait(barrier, chips + inner)

    def piece(c):
        return pl.ds(c * cut, cut)

    def send(c, slot, origin, target, source):
        return pltpu.make_async_remote_copy(
            src_ref=source.at[:, :, piece(c)],
            dst_ref=whole.at[origin, :, :, piece(c)],
            send_sem=send_sem.at[c, slot],
            recv_sem=recv_sem.at[c, origin],
            device_id={"tgt": target},
            device_id_type=MESH,
        )

    def arrived(c, origin):
        send(c, 0, origin, mate, src).wait_recv()

    sent = []
    for c in range(chunks):
        for step in range(1, chips):
            sent.append(send(c, step, me, peer(step), src))
            sent[-1].start()
        sent.append(send(c, 0, me, mate, src))
        sent[-1].start()
    own.wait()

    def source_block(p, cols):
        return jnp.concatenate([whole[t, p, :, cols] for t in range(nt)], axis=0)

    def columns(j):
        return pl.ds(pl.multiple_of(j * LANES, LANES), LANES)

    def forward_block(j, carry):
        cols = columns(j)
        target = tgt[0, :, cols]
        pair = jnp.concatenate([target * source_block(p, cols) for p in range(count)], axis=1)
        value = from_right(from_left(left_f[...], pair), right_fh[...], right_fl[...])
        for y in range(fold):
            at = pl.multiple_of((j * fold + y) * size, size)
            field[pl.ds(at, size), :] = value[:, y * count * size:(y + 1) * count * size]
        return carry

    def partner_arrived(c):
        arrived(c, mate)
        for step in range(1, chips):
            arrived(c, lax.rem(chip + step, chips) * 2 + 1 - core)

    for c in range(chunks + 1):
        if c < chunks:
            for step in range(1, chips):
                origin = peer(-step)
                arrived(c, origin)
                sent.append(send(c, chips - 1 + step, origin, mate, whole.at[origin]))
                sent[-1].start()
        if c > 0:
            partner_arrived(c - 1)
            lax.fori_loop((c - 1) * blocks, c * blocks, forward_block, 0)

    def middle(k, carry):
        first = k * 2
        value = jnp.concatenate(
            [field[pl.ds(first + i, size, stride=size), :] for i in range(2)], axis=1)
        scale = []
        for i in range(2):
            index = first + i
            scale.append(kern[jnp.where(index > size // 2, index - size // 2, index)])
        value = from_left(left_f[...], value) * jnp.concatenate(scale, axis=1)
        value = from_left(left_i[...], value)
        for i in range(2):
            lanes = count * size
            field[pl.ds(first + i, size, stride=size), :] = value[:, i * lanes:(i + 1) * lanes]
        return carry

    lax.fori_loop(0, size // 2, middle, 0)

    def inverse_block(j, carry):
        cols = columns(j)
        value = jnp.concatenate(
            [field[pl.ds(pl.multiple_of((j * fold + y) * size, size), size), :] for y in range(fold)], axis=1)
        value = from_left(left_i[...], from_right(value, right_ih[...], right_il[...]))
        total = None
        for p in range(count):
            term = (value[:, p * LANES:(p + 1) * LANES] * source_block(p, cols)) * occ[p]
            total = term if total is None else total + term
        total = -total
        for d in range(ns):
            part[d, :, cols] = total[d * rows:(d + 1) * rows, :]
        return carry

    order = []
    for d in range((ns + 1) // 2):
        order += [ns - 1 - d] + ([d] if d != ns - 1 - d else [])

    def pass_on(c, d, upward):
        buffer, sems = (from_low, low_recv) if upward else (from_high, high_recv)
        return pltpu.make_async_remote_copy(
            src_ref=part.at[d, :, piece(c)],
            dst_ref=buffer.at[d, :, piece(c)],
            send_sem=sum_send.at[c, d],
            recv_sem=sems.at[c, d],
            device_id={"src": here + 1 if upward else here - 1},
            device_id_type=MESH,
        )

    def start_ends(c):
        for d in order:
            if d > 0:
                @pl.when(here == 0)
                def _():
                    pass_on(c, d, True).start()
            if d < ns - 1:
                @pl.when(here == ns - 1)
                def _():
                    pass_on(c, d, False).start()

    def relay(c):
        for d in order:
            if d > 1:
                @pl.when((here > 0) & (here < d))
                def _():
                    pass_on(c, d, True).wait_recv()
                    part[d, :, piece(c)] += from_low[d, :, piece(c)]
                    pass_on(c, d, True).start()
            if d < ns - 2:
                @pl.when((here < ns - 1) & (here > d))
                def _():
                    pass_on(c, d, False).wait_recv()
                    part[d, :, piece(c)] += from_high[d, :, piece(c)]
                    pass_on(c, d, False).start()

    def finish(c):
        out[0, :, piece(c)] = part[here, :, piece(c)]

        @pl.when(here > 0)
        def _():
            pass_on(c, here, True).wait_recv()
            out[0, :, piece(c)] += from_low[here, :, piece(c)]

        @pl.when(here < ns - 1)
        def _():
            pass_on(c, here, False).wait_recv()
            out[0, :, piece(c)] += from_high[here, :, piece(c)]

    for c in range(chunks):
        lax.fori_loop(c * blocks, (c + 1) * blocks, inverse_block, 0)
        start_ends(c)
        if c > 0:
            relay(c - 1)
    relay(chunks - 1)
    for c in range(chunks):
        finish(c)

    for copy in sent:
        copy.wait_send()
    for c in range(chunks):
        for d in range(ns):
            @pl.when(here != d)
            def _():
                pass_on(c, d, True).wait_send()


def on_device(nt, ns, targets, sources, occupations):
    size, width = targets.shape[1], targets.shape[2]
    count, slab = sources.shape[0], sources.shape[1]
    rows = size // ns
    chunks = 4
    consts = [jnp.asarray(t) for t in tables(size, count)]
    vmem = pl.BlockSpec(memory_space=pltpu.VMEM)
    smem = pl.BlockSpec(memory_space=pltpu.SMEM)
    return pl.pallas_call(
        functools.partial(body, (nt, ns, count, size, chunks)),
        out_shape=jax.ShapeDtypeStruct((1, rows, width), jnp.float32),
        in_specs=[vmem, vmem, smem] + [vmem] * len(consts),
        out_specs=vmem,
        scratch_shapes=[
            pltpu.VMEM((nt, count, slab, width), jnp.float32),
            pltpu.VMEM((size * size, count * size), jnp.float32),
            pltpu.VMEM((ns, rows, width), jnp.float32),
            pltpu.VMEM((ns, rows, width), jnp.float32),
            pltpu.VMEM((ns, rows, width), jnp.float32),
            pltpu.SemaphoreType.DMA,
            pltpu.SemaphoreType.DMA((chunks, nt)),
            pltpu.SemaphoreType.DMA((chunks, nt)),
            pltpu.SemaphoreType.DMA((chunks, ns)),
            pltpu.SemaphoreType.DMA((chunks, ns)),
            pltpu.SemaphoreType.DMA((chunks, ns)),
        ],
        compiler_params=pltpu.CompilerParams(
            collective_id=0, has_side_effects=True, vmem_limit_bytes=48 * 1024 * 1024
        ),
    )(targets, sources, occupations, *consts)


def solution(mesh):
    return jax.shard_map(
        functools.partial(on_device, mesh.shape["tgt"], mesh.shape["src"]),
        mesh=mesh,
        in_specs=(P("tgt", None, None), P("src", "tgt", None), P("src")),
        out_specs=P("tgt", "src", None),
        check_vma=False,
    )
```

```python
import functools
import math

import jax
import jax.numpy as jnp
import ml_dtypes
import numpy as np
from jax import lax
from jax.experimental import pallas as pl
from jax.experimental.pallas import tpu as pltpu
from jax.sharding import PartitionSpec as P

MESH = pl.DeviceIdType.MESH
LANES = 128
CHUNKS = 4
BATCH = 8
GROUP = 16


def split_table(table):
    high = table.astype(np.float32).astype(ml_dtypes.bfloat16)
    low = (table - high.astype(np.float64)).astype(np.float32).astype(ml_dtypes.bfloat16)
    return high, low


def basis(size):
    half = size // 2
    point = np.arange(size)
    freq = np.where(point <= half, point, point - half)
    angle = (freq[:, None] * point[None, :] % size) * (2.0 * math.pi / size)
    rows = np.where((point <= half)[:, None], np.cos(angle), np.sin(angle))
    norm = np.where((freq == 0) | (freq == half), 1.0, 2.0) / size
    return rows * np.sqrt(norm)[:, None], freq


def tables(size, count):
    rows, freq = basis(size)
    fold = LANES // size

    def left(matrix):
        high, low = split_table(matrix)
        return np.concatenate([high, high, low], axis=1)

    wide = np.zeros((count, fold, size, fold, count, size))
    for p in range(count):
        for y in range(fold):
            wide[p, y, :, y, p, :] = rows.T
    wide = wide.reshape(count * LANES, count * LANES)
    half = np.arange(size // 2 + 1).astype(np.float64)
    square = half[:, None, None] ** 2 + freq[None, :, None] ** 2 + freq[None, None, :] ** 2
    kern = (16.0 / (square + 0.25)).astype(np.float32)
    kern = np.concatenate([kern] * count, axis=-1)
    forward, inverse = split_table(wide), split_table(wide.T.copy())
    lefts = np.stack([left(rows), left(rows.T.copy())])
    return lefts, np.stack([*forward, *inverse]), kern


def halves(value):
    high = value.astype(jnp.bfloat16)
    low = (value - high.astype(jnp.float32)).astype(jnp.bfloat16)
    return high, low


def dot(a, b):
    return jnp.dot(a, b, preferred_element_type=jnp.float32)


def from_left(table, value):
    high, low = halves(value)
    return dot(table, jnp.concatenate([high, low, high], axis=0))


def from_right(value, table_high, table_low):
    high, low = halves(value)
    return dot(high, table_high) + dot(low, table_high) + dot(high, table_low)


def body(shape, tgt_any, src_any, occ, left_any, right_any, kern_any, out,
         tgt, left, right, kern, load_sem, whole, field, part, inbox, relay, own_sem, send_sem, recv_sem, sum_send, sum_recv, relay_recv):
    nt, ns, count, size, chunks = shape
    width = size * size
    cut = width // chunks
    batch = math.gcd(BATCH, cut // LANES)
    loops = cut // LANES // batch
    group = math.gcd(GROUP, size)
    fold = LANES // size
    rows = part.shape[1]
    me, here = lax.axis_index("tgt"), lax.axis_index("src")
    chips = nt // 2
    chip, core = me // 2, me % 2
    mate = chip * 2 + (1 - core)

    def peer(step):
        return lax.rem(chip + step + chips, chips) * 2 + core

    barrier = pltpu.get_barrier_semaphore()
    for step in range(1, chips):
        pl.semaphore_signal(barrier, inc=1, device_id={"tgt": peer(step)}, device_id_type=MESH)
    pl.semaphore_signal(barrier, inc=1, device_id={"tgt": mate}, device_id_type=MESH)

    for step in range(1, ns):
        pl.semaphore_signal(barrier, inc=1, device_id={"src": lax.rem(here + step, ns)}, device_id_type=MESH)

    own = pltpu.make_async_copy(src_any, whole.at[me], own_sem)
    own.start()
    src = whole.at[me]
    loads = [
        pltpu.make_async_copy(here_ref, there_ref, load_sem.at[i])
        for i, (here_ref, there_ref) in enumerate(
            [(left_any, left), (right_any, right), (tgt_any, tgt), (kern_any, kern)])
    ]
    for load in loads:
        load.start()
    pl.semaphore_wait(barrier, chips + ns - 1)

    def piece(c):
        return pl.ds(c * cut, cut)

    def send(c, slot, origin, target, source):
        return pltpu.make_async_remote_copy(
            src_ref=source.at[:, :, piece(c)],
            dst_ref=whole.at[origin, :, :, piece(c)],
            send_sem=send_sem.at[c, slot],
            recv_sem=recv_sem.at[c, origin],
            device_id={"tgt": target},
            device_id_type=MESH,
        )

    def arrived(c, origin):
        send(c, 0, origin, mate, src).wait_recv()

    own.wait()
    sent = []
    for c in range(chunks):
        for step in range(1, chips):
            sent.append(send(c, step, me, peer(step), src))
            sent[-1].start()
        sent.append(send(c, 0, me, mate, src))
        sent[-1].start()
    for load in loads[:3]:
        load.wait()

    def source_block(p, cols):
        return jnp.concatenate([whole[t, p, :, cols] for t in range(nt)], axis=0)

    def columns(j):
        return pl.ds(pl.multiple_of(j * LANES, LANES), LANES)

    def stacked(value):
        wide = count * LANES
        return jnp.concatenate([value[:, b * wide:(b + 1) * wide] for b in range(batch)], axis=0)

    def unstacked(value):
        return jnp.concatenate([value[b * size:(b + 1) * size] for b in range(batch)], axis=1)

    def forward_blocks(i, carry):
        pairs = []
        for b in range(batch):
            cols = columns(i * batch + b)
            target = tgt[0, :, cols]
            pairs += [target * source_block(p, cols) for p in range(count)]
        value = stacked(from_left(left[0], jnp.concatenate(pairs, axis=1)))
        value = from_right(value, right[0], right[1])
        for b in range(batch):
            for y in range(fold):
                at = pl.multiple_of(((i * batch + b) * fold + y) * size, size)
                field[pl.ds(at, size), :] = value[
                    b * size:(b + 1) * size, y * count * size:(y + 1) * count * size]
        return carry

    def partner_arrived(c):
        arrived(c, mate)
        for step in range(1, chips):
            arrived(c, lax.rem(chip + step, chips) * 2 + 1 - core)

    for c in range(chunks + 1):
        if c < chunks:
            for step in range(1, chips):
                origin = peer(-step)
                arrived(c, origin)
                sent.append(send(c, chips - 1 + step, origin, mate, whole.at[origin]))
                sent[-1].start()
        if c > 0:
            partner_arrived(c - 1)
            lax.fori_loop((c - 1) * loops, c * loops, forward_blocks, 0)

    def middle(k, carry):
        lanes = count * size
        first = k * group
        value = jnp.concatenate(
            [field[pl.ds(first + i, size, stride=size), :] for i in range(group)], axis=1)
        scale = []
        for i in range(group):
            index = first + i
            scale.append(kern[jnp.where(index > size // 2, index - size // 2, index)])
        value = from_left(left[0], value) * jnp.concatenate(scale, axis=1)
        value = from_left(left[1], value)
        for i in range(group):
            field[pl.ds(first + i, size, stride=size), :] = value[:, i * lanes:(i + 1) * lanes]
        return carry

    loads[3].wait()
    lax.fori_loop(0, size // group, middle, 0)

    def inverse_blocks(i, carry):
        value = jnp.concatenate([
            jnp.concatenate([
                field[pl.ds(pl.multiple_of(((i * batch + b) * fold + y) * size, size), size), :]
                for y in range(fold)], axis=1)
            for b in range(batch)], axis=0)
        value = from_left(left[1], unstacked(from_right(value, right[2], right[3])))
        for b in range(batch):
            cols = columns(i * batch + b)
            total = None
            for p in range(count):
                at = (b * count + p) * LANES
                term = value[:, at:at + LANES] * source_block(p, cols) * occ[p]
                total = term if total is None else total + term
            total = -total
            for d in range(ns):
                part[d, :, cols] = total[d * rows:(d + 1) * rows, :]
        return carry

    relayed = ns >= 4
    last = ns - 1

    def term(c, d):
        return pltpu.make_async_remote_copy(
            src_ref=part.at[d, :, piece(c)],
            dst_ref=inbox.at[here, :, piece(c)],
            send_sem=sum_send.at[c, d],
            recv_sem=sum_recv.at[c, here],
            device_id={"src": d},
            device_id_type=MESH,
        )

    def term_arrived(c, origin):
        pltpu.make_async_remote_copy(
            src_ref=part.at[0, :, piece(c)],
            dst_ref=inbox.at[origin, :, piece(c)],
            send_sem=sum_send.at[c, 0],
            recv_sem=sum_recv.at[c, origin],
            device_id={"src": origin},
            device_id_type=MESH,
        ).wait_recv()

    def far(c, upward):
        return pltpu.make_async_remote_copy(
            src_ref=part.at[last if upward else 0, :, piece(c)],
            dst_ref=relay.at[:, piece(c)],
            send_sem=sum_send.at[c, last if upward else 0],
            recv_sem=relay_recv.at[c],
            device_id={"src": 1 if upward else last - 1},
            device_id_type=MESH,
        )

    def start_far(c):
        if relayed:
            for end in (0, last):
                @pl.when(here == end)
                def _():
                    far(c, end == 0).start()

    def start_near(c, s):
        order = sorted((d for d in range(ns) if d != s), key=lambda d: -abs(d - s))
        for d in order:
            if not (relayed and (d == last and s in (0, 1) or d == 0 and s in (last, last - 1))):
                term(c, d).start()

    def start_relay(c):
        if relayed:
            for s, d in ((1, last), (last - 1, 0)):
                @pl.when(here == s)
                def _():
                    far(c, s == 1).wait_recv()
                    part[d, :, piece(c)] += relay[:, piece(c)]
                    term(c, d).start()

    def middles(c):
        for s in range(1, last):
            @pl.when(here == s)
            def _():
                start_near(c, s)

    def ends(c):
        for s in (0, last):
            @pl.when(here == s)
            def _():
                start_near(c, s)

    def finish(c):
        out[0, :, piece(c)] = part[here, :, piece(c)]
        for o in range(ns):
            there = here != o
            if relayed and o in (0, last):
                there = there & (here != last - o)

            @pl.when(there)
            def _():
                term_arrived(c, o)
                out[0, :, piece(c)] += inbox[o, :, piece(c)]

    for c in range(chunks):
        lax.fori_loop(c * loops, (c + 1) * loops, inverse_blocks, 0)
        start_far(c)
        middles(c)
        if c > 0:
            ends(c - 1)
            start_relay(c - 1)
    ends(chunks - 1)
    start_relay(chunks - 1)
    for c in range(chunks):
        finish(c)

    for copy in sent:
        copy.wait_send()
    for c in range(chunks):
        for d in range(ns):
            @pl.when(here != d)
            def _():
                term(c, d).wait_send()


def on_device(nt, ns, targets, sources, occupations):
    size, width = targets.shape[1], targets.shape[2]
    count, slab = sources.shape[0], sources.shape[1]
    rows = size // ns
    chunks = CHUNKS
    consts = [jnp.asarray(t) for t in tables(size, count)]
    vmem = pl.BlockSpec(memory_space=pltpu.VMEM)
    hbm = pl.BlockSpec(memory_space=pl.ANY)
    smem = pl.BlockSpec(memory_space=pltpu.SMEM)
    return pl.pallas_call(
        functools.partial(body, (nt, ns, count, size, chunks)),
        out_shape=jax.ShapeDtypeStruct((1, rows, width), jnp.float32),
        in_specs=[hbm, hbm, smem] + [hbm] * len(consts),
        out_specs=vmem,
        scratch_shapes=[
            pltpu.VMEM(targets.shape, jnp.float32),
            *(pltpu.VMEM(t.shape, t.dtype) for t in consts),
            pltpu.SemaphoreType.DMA((1 + len(consts),)),
            pltpu.VMEM((nt, count, slab, width), jnp.float32),
            pltpu.VMEM((size * size, count * size), jnp.float32),
            pltpu.VMEM((ns, rows, width), jnp.float32),
            pltpu.VMEM((ns, rows, width), jnp.float32),
            pltpu.VMEM((rows, width), jnp.float32),
            pltpu.SemaphoreType.DMA,
            pltpu.SemaphoreType.DMA((chunks, nt)),
            pltpu.SemaphoreType.DMA((chunks, nt)),
            pltpu.SemaphoreType.DMA((chunks, ns)),
            pltpu.SemaphoreType.DMA((chunks, ns)),
            pltpu.SemaphoreType.DMA((chunks,)),
        ],
        compiler_params=pltpu.CompilerParams(
            collective_id=0, has_side_effects=True, vmem_limit_bytes=63 * 1024 * 1024
        ),
    )(targets, sources, occupations, *consts)


def solution(mesh):
    return jax.shard_map(
        functools.partial(on_device, mesh.shape["tgt"], mesh.shape["src"]),
        mesh=mesh,
        in_specs=(P("tgt", None, None), P("src", "tgt", None), P("src")),
        out_specs=P("tgt", "src", None),
        check_vma=False,
    )
```

```python
import functools
import math

import jax
import jax.numpy as jnp
import ml_dtypes
import numpy as np
from jax import lax
from jax.experimental import pallas as pl
from jax.experimental.pallas import tpu as pltpu
from jax.sharding import PartitionSpec as P

MESH = pl.DeviceIdType.MESH
LANES = 128
CHUNKS = 4
BATCH = 8
GROUP = 16


def split_table(table):
    high = table.astype(np.float32).astype(ml_dtypes.bfloat16)
    low = (table - high.astype(np.float64)).astype(np.float32).astype(ml_dtypes.bfloat16)
    return high, low


def basis(size):
    half = size // 2
    point = np.arange(size)
    freq = np.where(point <= half, point, point - half)
    angle = (freq[:, None] * point[None, :] % size) * (2.0 * math.pi / size)
    rows = np.where((point <= half)[:, None], np.cos(angle), np.sin(angle))
    norm = np.where((freq == 0) | (freq == half), 1.0, 2.0) / size
    return rows * np.sqrt(norm)[:, None], freq


def tables(size, count):
    rows, freq = basis(size)
    fold = LANES // size

    def left(matrix):
        high, low = split_table(matrix)
        return np.concatenate([high, high, low], axis=1)

    wide = np.zeros((count, fold, size, fold, count, size))
    for p in range(count):
        for y in range(fold):
            wide[p, y, :, y, p, :] = rows.T
    wide = wide.reshape(count * LANES, count * LANES)
    half = np.arange(size // 2 + 1).astype(np.float64)
    square = half[:, None, None] ** 2 + freq[None, :, None] ** 2 + freq[None, None, :] ** 2
    kern = (16.0 / (square + 0.25)).astype(np.float32)
    kern = np.concatenate([kern] * count, axis=-1)
    forward, inverse = split_table(wide), split_table(wide.T.copy())
    lefts = np.stack([left(rows), left(rows.T.copy())])
    return lefts, np.stack([*forward, *inverse]), kern


def halves(value):
    high = value.astype(jnp.bfloat16)
    low = (value - high.astype(jnp.float32)).astype(jnp.bfloat16)
    return high, low


def dot(a, b):
    return jnp.dot(a, b, preferred_element_type=jnp.float32)


def from_left(table, value):
    high, low = halves(value)
    return dot(table, jnp.concatenate([high, low, high], axis=0))


def from_right(value, table_high, table_low):
    high, low = halves(value)
    return dot(high, table_high) + dot(low, table_high) + dot(high, table_low)


def body(shape, tgt_any, src_any, occ, left_any, right_any, kern_any, out,
         tgt, left, right, kern, load_sem, whole, field, part, inbox, relay, own_sem, send_sem, recv_sem, sum_send, sum_recv, relay_recv):
    nt, ns, count, size, chunks = shape
    width = size * size
    cut = width // chunks
    batch = math.gcd(BATCH, cut // LANES)
    loops = cut // LANES // batch
    group = math.gcd(GROUP, size)
    fold = LANES // size
    rows = part.shape[1]
    me, here = lax.axis_index("tgt"), lax.axis_index("src")
    chips = nt // 2
    chip, core = me // 2, me % 2
    mate = chip * 2 + (1 - core)

    def peer(step):
        return lax.rem(chip + step + chips, chips) * 2 + core

    barrier = pltpu.get_barrier_semaphore()
    for step in range(1, chips):
        pl.semaphore_signal(barrier, inc=1, device_id={"tgt": peer(step)}, device_id_type=MESH)
    pl.semaphore_signal(barrier, inc=1, device_id={"tgt": mate}, device_id_type=MESH)

    for step in range(1, ns):
        pl.semaphore_signal(barrier, inc=1, device_id={"src": lax.rem(here + step, ns)}, device_id_type=MESH)

    own = pltpu.make_async_copy(src_any, whole.at[me], own_sem)
    own.start()
    src = whole.at[me]
    loads = [
        pltpu.make_async_copy(here_ref, there_ref, load_sem.at[i])
        for i, (here_ref, there_ref) in enumerate(
            [(left_any, left), (right_any, right), (tgt_any, tgt), (kern_any, kern)])
    ]
    for load in loads:
        load.start()
    pl.semaphore_wait(barrier, chips + ns - 1)

    def piece(c):
        return pl.ds(c * cut, cut)

    across, beyond, corner = chip + 1 - 2 * (chip % 2), lax.rem(chip + 2, 4), 3 - chip
    folded = chips == 4
    near, rest = (0, (count + 1) // 2), ((count + 1) // 2, count - (count + 1) // 2)
    all_of = (0, count)

    def copy_of(c, out_slot, in_slot, origin, target, source, span):
        return pltpu.make_async_remote_copy(
            src_ref=source.at[pl.ds(*span), :, piece(c)],
            dst_ref=whole.at[origin, pl.ds(*span), :, piece(c)],
            send_sem=send_sem.at[c, out_slot],
            recv_sem=recv_sem.at[c, in_slot],
            device_id={"tgt": target},
            device_id_type=MESH,
        )

    sent = []

    def send(c, out_slot, in_slot, origin, target, source, span=all_of):
        sent.append(copy_of(c, out_slot, in_slot, origin, target, source, span))
        sent[-1].start()

    def arrived(c, in_slot, origin, span=all_of):
        copy_of(c, 0, in_slot, origin, mate, whole.at[origin], span).wait_recv()

    def at(place):
        return place * 2 + core

    def beside(place):
        return place * 2 + 1 - core

    def first_hop(c):
        if folded:
            send(c, 0, 0, me, at(across), src)
            send(c, 1, 1, me, at(beyond), src)
            send(c, 2, 4, me, mate, src)
        else:
            for step in range(1, chips):
                send(c, step, me, me, peer(step), src)
            send(c, 0, me, me, mate, src)

    def second_hop(c):
        if folded:
            arrived(c, 0, at(across))
            send(c, 3, 2, at(across), at(beyond), whole.at[at(across)], near)
            arrived(c, 1, at(beyond))
            send(c, 4, 3, at(beyond), at(across), whole.at[at(beyond)], rest)
            send(c, 5, 5, at(across), mate, whole.at[at(across)])
            send(c, 6, 6, at(beyond), mate, whole.at[at(beyond)])
        else:
            for step in range(1, chips):
                origin = peer(-step)
                arrived(c, origin, origin)
                send(c, chips - 1 + step, origin, origin, mate, whole.at[origin])

    def third_hop(c):
        if folded:
            arrived(c, 2, at(corner), near)
            arrived(c, 3, at(corner), rest)
            send(c, 7, 7, at(corner), mate, whole.at[at(corner)])

    def complete(c):
        if folded:
            arrived(c, 4, mate)
            arrived(c, 5, beside(across))
            arrived(c, 6, beside(beyond))
            arrived(c, 7, beside(corner))
        else:
            arrived(c, mate, mate)
            for step in range(1, chips):
                origin = beside(lax.rem(chip + step, chips))
                arrived(c, origin, origin)

    own.wait()
    for c in range(chunks):
        first_hop(c)
    for load in loads[:3]:
        load.wait()

    def source_block(p, cols):
        return jnp.concatenate([whole[t, p, :, cols] for t in range(nt)], axis=0)

    def columns(j):
        return pl.ds(pl.multiple_of(j * LANES, LANES), LANES)

    def stacked(value):
        wide = count * LANES
        return jnp.concatenate([value[:, b * wide:(b + 1) * wide] for b in range(batch)], axis=0)

    def unstacked(value):
        return jnp.concatenate([value[b * size:(b + 1) * size] for b in range(batch)], axis=1)

    def forward_blocks(i, carry):
        pairs = []
        for b in range(batch):
            cols = columns(i * batch + b)
            target = tgt[0, :, cols]
            pairs += [target * source_block(p, cols) for p in range(count)]
        value = stacked(from_left(left[0], jnp.concatenate(pairs, axis=1)))
        value = from_right(value, right[0], right[1])
        for b in range(batch):
            for y in range(fold):
                row = pl.multiple_of(((i * batch + b) * fold + y) * size, size)
                field[pl.ds(row, size), :] = value[
                    b * size:(b + 1) * size, y * count * size:(y + 1) * count * size]
        return carry

    for step in range(chunks + 2):
        if step < chunks:
            second_hop(step)
        if step >= 2:
            complete(step - 2)
            lax.fori_loop((step - 2) * loops, (step - 1) * loops, forward_blocks, 0)
        if 1 <= step <= chunks:
            third_hop(step - 1)

    def middle(k, carry):
        lanes = count * size
        first = k * group
        value = jnp.concatenate(
            [field[pl.ds(first + i, size, stride=size), :] for i in range(group)], axis=1)
        scale = []
        for i in range(group):
            index = first + i
            scale.append(kern[jnp.where(index > size // 2, index - size // 2, index)])
        value = from_left(left[0], value) * jnp.concatenate(scale, axis=1)
        value = from_left(left[1], value)
        for i in range(group):
            field[pl.ds(first + i, size, stride=size), :] = value[:, i * lanes:(i + 1) * lanes]
        return carry

    loads[3].wait()
    lax.fori_loop(0, size // group, middle, 0)

    def inverse_blocks(i, carry):
        value = jnp.concatenate([
            jnp.concatenate([
                field[pl.ds(pl.multiple_of(((i * batch + b) * fold + y) * size, size), size), :]
                for y in range(fold)], axis=1)
            for b in range(batch)], axis=0)
        value = from_left(left[1], unstacked(from_right(value, right[2], right[3])))
        for b in range(batch):
            cols = columns(i * batch + b)
            total = None
            for p in range(count):
                lane = (b * count + p) * LANES
                term = value[:, lane:lane + LANES] * source_block(p, cols) * occ[p]
                total = term if total is None else total + term
            total = -total
            for d in range(ns):
                part[d, :, cols] = total[d * rows:(d + 1) * rows, :]
        return carry

    relayed = ns >= 4
    last = ns - 1

    def term(c, d):
        return pltpu.make_async_remote_copy(
            src_ref=part.at[d, :, piece(c)],
            dst_ref=inbox.at[here, :, piece(c)],
            send_sem=sum_send.at[c, d],
            recv_sem=sum_recv.at[c, here],
            device_id={"src": d},
            device_id_type=MESH,
        )

    def term_arrived(c, origin):
        pltpu.make_async_remote_copy(
            src_ref=part.at[0, :, piece(c)],
            dst_ref=inbox.at[origin, :, piece(c)],
            send_sem=sum_send.at[c, 0],
            recv_sem=sum_recv.at[c, origin],
            device_id={"src": origin},
            device_id_type=MESH,
        ).wait_recv()

    def far(c, upward):
        return pltpu.make_async_remote_copy(
            src_ref=part.at[last if upward else 0, :, piece(c)],
            dst_ref=relay.at[:, piece(c)],
            send_sem=sum_send.at[c, last if upward else 0],
            recv_sem=relay_recv.at[c],
            device_id={"src": 1 if upward else last - 1},
            device_id_type=MESH,
        )

    def start_far(c):
        if relayed:
            for end in (0, last):
                @pl.when(here == end)
                def _():
                    far(c, end == 0).start()

    def start_near(c, s):
        order = sorted((d for d in range(ns) if d != s), key=lambda d: -abs(d - s))
        for d in order:
            if not (relayed and (d == last and s in (0, 1) or d == 0 and s in (last, last - 1))):
                term(c, d).start()

    def start_relay(c):
        if relayed:
            for s, d in ((1, last), (last - 1, 0)):
                @pl.when(here == s)
                def _():
                    far(c, s == 1).wait_recv()
                    part[d, :, piece(c)] += relay[:, piece(c)]
                    term(c, d).start()

    def middles(c):
        for s in range(1, last):
            @pl.when(here == s)
            def _():
                start_near(c, s)

    def ends(c):
        for s in (0, last):
            @pl.when(here == s)
            def _():
                start_near(c, s)

    def finish(c):
        out[0, :, piece(c)] = part[here, :, piece(c)]
        for o in range(ns):
            there = here != o
            if relayed and o in (0, last):
                there = there & (here != last - o)

            @pl.when(there)
            def _():
                term_arrived(c, o)
                out[0, :, piece(c)] += inbox[o, :, piece(c)]

    for c in range(chunks):
        lax.fori_loop(c * loops, (c + 1) * loops, inverse_blocks, 0)
        start_far(c)
        middles(c)
        if c > 0:
            ends(c - 1)
            start_relay(c - 1)
    ends(chunks - 1)
    start_relay(chunks - 1)
    for c in range(chunks):
        finish(c)

    for copy in sent:
        copy.wait_send()
    for c in range(chunks):
        for d in range(ns):
            @pl.when(here != d)
            def _():
                term(c, d).wait_send()


def on_device(nt, ns, targets, sources, occupations):
    size, width = targets.shape[1], targets.shape[2]
    count, slab = sources.shape[0], sources.shape[1]
    rows = size // ns
    chunks = CHUNKS
    consts = [jnp.asarray(t) for t in tables(size, count)]
    vmem = pl.BlockSpec(memory_space=pltpu.VMEM)
    hbm = pl.BlockSpec(memory_space=pl.ANY)
    smem = pl.BlockSpec(memory_space=pltpu.SMEM)
    return pl.pallas_call(
        functools.partial(body, (nt, ns, count, size, chunks)),
        out_shape=jax.ShapeDtypeStruct((1, rows, width), jnp.float32),
        in_specs=[hbm, hbm, smem] + [hbm] * len(consts),
        out_specs=vmem,
        scratch_shapes=[
            pltpu.VMEM(targets.shape, jnp.float32),
            *(pltpu.VMEM(t.shape, t.dtype) for t in consts),
            pltpu.SemaphoreType.DMA((1 + len(consts),)),
            pltpu.VMEM((nt, count, slab, width), jnp.float32),
            pltpu.VMEM((size * size, count * size), jnp.float32),
            pltpu.VMEM((ns, rows, width), jnp.float32),
            pltpu.VMEM((ns, rows, width), jnp.float32),
            pltpu.VMEM((rows, width), jnp.float32),
            pltpu.SemaphoreType.DMA,
            pltpu.SemaphoreType.DMA((chunks, nt)),
            pltpu.SemaphoreType.DMA((chunks, nt)),
            pltpu.SemaphoreType.DMA((chunks, ns)),
            pltpu.SemaphoreType.DMA((chunks, ns)),
            pltpu.SemaphoreType.DMA((chunks,)),
        ],
        compiler_params=pltpu.CompilerParams(
            collective_id=0, has_side_effects=True, vmem_limit_bytes=63 * 1024 * 1024
        ),
    )(targets, sources, occupations, *consts)


def solution(mesh):
    return jax.shard_map(
        functools.partial(on_device, mesh.shape["tgt"], mesh.shape["src"]),
        mesh=mesh,
        in_specs=(P("tgt", None, None), P("src", "tgt", None), P("src")),
        out_specs=P("tgt", "src", None),
        check_vma=False,
    )
```

```python
import functools
import math

import jax
import jax.numpy as jnp
import ml_dtypes
import numpy as np
from jax import lax
from jax.experimental import pallas as pl
from jax.experimental.pallas import tpu as pltpu
from jax.sharding import PartitionSpec as P

MESH = pl.DeviceIdType.MESH
LANES = 128
CHUNKS = 4
GATHERS = 4
BATCH = 8
GROUP = 32


def split_table(table):
    high = table.astype(np.float32).astype(ml_dtypes.bfloat16)
    low = (table - high.astype(np.float64)).astype(np.float32).astype(ml_dtypes.bfloat16)
    return high, low


def basis(size):
    half = size // 2
    point = np.arange(size)
    freq = np.where(point <= half, point, point - half)
    angle = (freq[:, None] * point[None, :] % size) * (2.0 * math.pi / size)
    rows = np.where((point <= half)[:, None], np.cos(angle), np.sin(angle))
    norm = np.where((freq == 0) | (freq == half), 1.0, 2.0) / size
    return rows * np.sqrt(norm)[:, None], freq


def tables(size, count):
    rows, freq = basis(size)
    fold = LANES // size

    def left(matrix):
        high, low = split_table(matrix)
        return np.concatenate([high, high, low], axis=1)

    wide = np.zeros((count, fold, size, fold, count, size))
    for p in range(count):
        for y in range(fold):
            wide[p, y, :, y, p, :] = rows.T
    wide = wide.reshape(count * LANES, count * LANES)
    half = np.arange(size // 2 + 1).astype(np.float64)
    square = half[:, None, None] ** 2 + freq[None, :, None] ** 2 + freq[None, None, :] ** 2
    kern = (16.0 / (square + 0.25)).astype(np.float32)
    kern = np.concatenate([kern] * count, axis=-1)
    forward, inverse = split_table(wide), split_table(wide.T.copy())
    lefts = np.stack([left(rows), left(rows.T.copy())])
    return lefts, np.stack([*forward, *inverse]), kern


def halves(value):
    high = value.astype(jnp.bfloat16)
    low = (value - high.astype(jnp.float32)).astype(jnp.bfloat16)
    return high, low


def dot(a, b):
    return jnp.dot(a, b, preferred_element_type=jnp.float32)


def from_left(table, value):
    high, low = halves(value)
    return dot(table, jnp.concatenate([high, low, high], axis=0))


def from_right(value, table_high, table_low):
    high, low = halves(value)
    return dot(high, table_high) + dot(low, table_high) + dot(high, table_low)


def body(shape, tgt_any, src_any, occ, left_any, right_any, kern_any, out,
         tgt, left, right, kern, load_sem, whole, field, part, inbox, relay, own_sem, send_sem, recv_sem, sum_send, sum_recv, relay_recv):
    nt, ns, count, size, gathers, chunks = shape
    width = size * size
    cut = width // chunks
    batch = math.gcd(BATCH, cut // LANES)
    loops = cut // LANES // batch
    part_cut = width // gathers
    turns = part_cut // LANES // batch
    group = math.gcd(GROUP, size)
    fold = LANES // size
    rows = part.shape[1]
    me, here = lax.axis_index("tgt"), lax.axis_index("src")
    chips = nt // 2
    chip, core = me // 2, me % 2
    mate = chip * 2 + (1 - core)

    def peer(step):
        return lax.rem(chip + step + chips, chips) * 2 + core

    barrier = pltpu.get_barrier_semaphore()
    for step in range(1, chips):
        pl.semaphore_signal(barrier, inc=1, device_id={"tgt": peer(step)}, device_id_type=MESH)
    pl.semaphore_signal(barrier, inc=1, device_id={"tgt": mate}, device_id_type=MESH)

    for step in range(1, ns):
        pl.semaphore_signal(barrier, inc=1, device_id={"src": lax.rem(here + step, ns)}, device_id_type=MESH)

    own = pltpu.make_async_copy(src_any, whole.at[me], own_sem)
    own.start()
    src = src_any
    loads = [
        pltpu.make_async_copy(here_ref, there_ref, load_sem.at[i])
        for i, (here_ref, there_ref) in enumerate(
            [(left_any, left), (right_any, right), (tgt_any, tgt), (kern_any, kern)])
    ]
    for load in loads:
        load.start()
    pl.semaphore_wait(barrier, chips + ns - 1)

    def strip(c):
        return pl.ds(c * part_cut, part_cut)

    def piece(c):
        return pl.ds(c * cut, cut)

    across, beyond, corner = chip + 1 - 2 * (chip % 2), lax.rem(chip + 2, 4), 3 - chip
    folded = chips == 4
    near, rest = (0, (count + 1) // 2), ((count + 1) // 2, count - (count + 1) // 2)
    all_of = (0, count)

    def copy_of(c, out_slot, in_slot, origin, target, source, span):
        return pltpu.make_async_remote_copy(
            src_ref=source.at[pl.ds(*span), :, strip(c)],
            dst_ref=whole.at[origin, pl.ds(*span), :, strip(c)],
            send_sem=send_sem.at[c, out_slot],
            recv_sem=recv_sem.at[c, in_slot],
            device_id={"tgt": target},
            device_id_type=MESH,
        )

    sent = []

    def send(c, out_slot, in_slot, origin, target, source, span=all_of):
        sent.append(copy_of(c, out_slot, in_slot, origin, target, source, span))
        sent[-1].start()

    def arrived(c, in_slot, origin, span=all_of):
        copy_of(c, 0, in_slot, origin, mate, whole.at[origin], span).wait_recv()

    def at(place):
        return place * 2 + core

    def beside(place):
        return place * 2 + 1 - core

    def first_hop(c):
        if folded:
            send(c, 0, 0, me, at(across), src)
            send(c, 1, 1, me, at(beyond), src)
            send(c, 2, 4, me, mate, src)
        else:
            for step in range(1, chips):
                send(c, step, me, me, peer(step), src)
            send(c, 0, me, me, mate, src)

    def second_hop(c):
        if folded:
            arrived(c, 0, at(across))
            send(c, 3, 2, at(across), at(beyond), whole.at[at(across)], near)
            arrived(c, 1, at(beyond))
            send(c, 4, 3, at(beyond), at(across), whole.at[at(beyond)], rest)
            send(c, 5, 5, at(across), mate, whole.at[at(across)])
            send(c, 6, 6, at(beyond), mate, whole.at[at(beyond)])
        else:
            for step in range(1, chips):
                origin = peer(-step)
                arrived(c, origin, origin)
                send(c, chips - 1 + step, origin, origin, mate, whole.at[origin])

    def third_hop(c):
        if folded:
            arrived(c, 2, at(corner), near)
            arrived(c, 3, at(corner), rest)
            send(c, 7, 7, at(corner), mate, whole.at[at(corner)])

    def complete(c):
        if folded:
            arrived(c, 4, mate)
            arrived(c, 5, beside(across))
            arrived(c, 6, beside(beyond))
            arrived(c, 7, beside(corner))
        else:
            arrived(c, mate, mate)
            for step in range(1, chips):
                origin = beside(lax.rem(chip + step, chips))
                arrived(c, origin, origin)

    for c in range(gathers):
        first_hop(c)
    own.wait()
    for load in loads[:3]:
        load.wait()

    def source_block(p, cols):
        return jnp.concatenate([whole[t, p, :, cols] for t in range(nt)], axis=0)

    def columns(j):
        return pl.ds(pl.multiple_of(j * LANES, LANES), LANES)

    def stacked(value):
        wide = count * LANES
        return jnp.concatenate([value[:, b * wide:(b + 1) * wide] for b in range(batch)], axis=0)

    def unstacked(value):
        return jnp.concatenate([value[b * size:(b + 1) * size] for b in range(batch)], axis=1)

    def forward_blocks(i, carry):
        pairs = []
        for b in range(batch):
            cols = columns(i * batch + b)
            target = tgt[0, :, cols]
            pairs += [target * source_block(p, cols) for p in range(count)]
        value = stacked(from_left(left[0], jnp.concatenate(pairs, axis=1)))
        value = from_right(value, right[0], right[1])
        for b in range(batch):
            for y in range(fold):
                row = pl.multiple_of(((i * batch + b) * fold + y) * size, size)
                field[pl.ds(row, size), :] = value[
                    b * size:(b + 1) * size, y * count * size:(y + 1) * count * size]
        return carry

    for step in range(gathers + 2):
        if step < gathers:
            second_hop(step)
        if step >= 2:
            complete(step - 2)
            lax.fori_loop((step - 2) * turns, (step - 1) * turns, forward_blocks, 0)
        if 1 <= step <= gathers:
            third_hop(step - 1)

    def middle(k, carry):
        lanes = count * size
        first = k * group
        value = jnp.concatenate(
            [field[pl.ds(first + i, size, stride=size), :] for i in range(group)], axis=1)
        scale = []
        for i in range(group):
            index = first + i
            scale.append(kern[jnp.where(index > size // 2, index - size // 2, index)])
        value = from_left(left[0], value) * jnp.concatenate(scale, axis=1)
        value = from_left(left[1], value)
        for i in range(group):
            field[pl.ds(first + i, size, stride=size), :] = value[:, i * lanes:(i + 1) * lanes]
        return carry

    loads[3].wait()
    lax.fori_loop(0, size // group, middle, 0)

    def inverse_blocks(i, carry):
        value = jnp.concatenate([
            jnp.concatenate([
                field[pl.ds(pl.multiple_of(((i * batch + b) * fold + y) * size, size), size), :]
                for y in range(fold)], axis=1)
            for b in range(batch)], axis=0)
        value = from_left(left[1], unstacked(from_right(value, right[2], right[3])))
        for b in range(batch):
            cols = columns(i * batch + b)
            total = None
            for p in range(count):
                lane = (b * count + p) * LANES
                term = value[:, lane:lane + LANES] * source_block(p, cols) * occ[p]
                total = term if total is None else total + term
            total = -total
            for d in range(ns):
                part[d, :, cols] = total[d * rows:(d + 1) * rows, :]
        return carry

    relayed = ns >= 4
    last = ns - 1

    def term(c, d):
        return pltpu.make_async_remote_copy(
            src_ref=part.at[d, :, piece(c)],
            dst_ref=inbox.at[here, :, piece(c)],
            send_sem=sum_send.at[c, d],
            recv_sem=sum_recv.at[c, here],
            device_id={"src": d},
            device_id_type=MESH,
        )

    def term_arrived(c, origin):
        pltpu.make_async_remote_copy(
            src_ref=part.at[0, :, piece(c)],
            dst_ref=inbox.at[origin, :, piece(c)],
            send_sem=sum_send.at[c, 0],
            recv_sem=sum_recv.at[c, origin],
            device_id={"src": origin},
            device_id_type=MESH,
        ).wait_recv()

    def far(c, upward):
        return pltpu.make_async_remote_copy(
            src_ref=part.at[last if upward else 0, :, piece(c)],
            dst_ref=relay.at[:, piece(c)],
            send_sem=sum_send.at[c, last if upward else 0],
            recv_sem=relay_recv.at[c],
            device_id={"src": 1 if upward else last - 1},
            device_id_type=MESH,
        )

    def start_far(c):
        if relayed:
            for end in (0, last):
                @pl.when(here == end)
                def _():
                    far(c, end == 0).start()

    def start_near(c, s):
        order = sorted((d for d in range(ns) if d != s), key=lambda d: -abs(d - s))
        for d in order:
            if not (relayed and (d == last and s in (0, 1) or d == 0 and s in (last, last - 1))):
                term(c, d).start()

    def start_relay(c):
        if relayed:
            for s, d in ((1, last), (last - 1, 0)):
                @pl.when(here == s)
                def _():
                    far(c, s == 1).wait_recv()
                    part[d, :, piece(c)] += relay[:, piece(c)]
                    term(c, d).start()

    def middles(c):
        for s in range(1, last):
            @pl.when(here == s)
            def _():
                start_near(c, s)

    def ends(c):
        for s in (0, last):
            @pl.when(here == s)
            def _():
                start_near(c, s)

    def finish(c):
        out[0, :, piece(c)] = part[here, :, piece(c)]
        for o in range(ns):
            there = here != o
            if relayed and o in (0, last):
                there = there & (here != last - o)

            @pl.when(there)
            def _():
                term_arrived(c, o)
                out[0, :, piece(c)] += inbox[o, :, piece(c)]

    for c in range(chunks):
        lax.fori_loop(c * loops, (c + 1) * loops, inverse_blocks, 0)
        start_far(c)
        middles(c)
        if c > 0:
            ends(c - 1)
            start_relay(c - 1)
    ends(chunks - 1)
    start_relay(chunks - 1)
    for c in range(chunks):
        finish(c)

    for copy in sent:
        copy.wait_send()
    for c in range(chunks):
        for d in range(ns):
            @pl.when(here != d)
            def _():
                term(c, d).wait_send()


def on_device(nt, ns, targets, sources, occupations):
    size, width = targets.shape[1], targets.shape[2]
    count, slab = sources.shape[0], sources.shape[1]
    rows = size // ns
    gathers, chunks = GATHERS, CHUNKS
    consts = [jnp.asarray(t) for t in tables(size, count)]
    vmem = pl.BlockSpec(memory_space=pltpu.VMEM)
    hbm = pl.BlockSpec(memory_space=pl.ANY)
    smem = pl.BlockSpec(memory_space=pltpu.SMEM)
    return pl.pallas_call(
        functools.partial(body, (nt, ns, count, size, gathers, chunks)),
        out_shape=jax.ShapeDtypeStruct((1, rows, width), jnp.float32),
        in_specs=[hbm, hbm, smem] + [hbm] * len(consts),
        out_specs=vmem,
        scratch_shapes=[
            pltpu.VMEM(targets.shape, jnp.float32),
            *(pltpu.VMEM(t.shape, t.dtype) for t in consts),
            pltpu.SemaphoreType.DMA((1 + len(consts),)),
            pltpu.VMEM((nt, count, slab, width), jnp.float32),
            pltpu.VMEM((size * size, count * size), jnp.float32),
            pltpu.VMEM((ns, rows, width), jnp.float32),
            pltpu.VMEM((ns, rows, width), jnp.float32),
            pltpu.VMEM((rows, width), jnp.float32),
            pltpu.SemaphoreType.DMA,
            pltpu.SemaphoreType.DMA((gathers, nt)),
            pltpu.SemaphoreType.DMA((gathers, nt)),
            pltpu.SemaphoreType.DMA((chunks, ns)),
            pltpu.SemaphoreType.DMA((chunks, ns)),
            pltpu.SemaphoreType.DMA((chunks,)),
        ],
        compiler_params=pltpu.CompilerParams(
            collective_id=0, has_side_effects=True, vmem_limit_bytes=63 * 1024 * 1024
        ),
    )(targets, sources, occupations, *consts)


def solution(mesh):
    return jax.shard_map(
        functools.partial(on_device, mesh.shape["tgt"], mesh.shape["src"]),
        mesh=mesh,
        in_specs=(P("tgt", None, None), P("src", "tgt", None), P("src")),
        out_specs=P("tgt", "src", None),
        check_vma=False,
    )
```
